256 devices in a mesh: section: 8 (over x, core), node: 4 (over z_lo), local: 8 (over z_hi, y).
Axes of the slice: x: 4, y: 4, z: 8 (z_hi: 2, z_lo: 4; z = z_hi * 4 + z_lo), core: 2. Of those that a mesh axis runs over, the one named last changes fastest.
Arguments:
- x_fwd: bfloat16 [8, 2048, 3584], P('section', ('node', 'local')), may hold values from -6 to 6
- route_fwd: int32 [8, 2048, 2], P('section', ('node', 'local')), may hold values from 0 to 3, all different within a row; in each aligned block of 64 rows (0 to 63, 64 to 127, ..., all dimensions but the last counted through in order) at most 36 rows name the same one
- weight_fwd: float32 [8, 2048, 2], P('section', ('node', 'local')), may hold values from 0.2 to 1.2
- x_bwd: bfloat16 [8, 2048, 3584], P('section', ('node', 'local')), may hold values from -6 to 6
- grad_out: bfloat16 [8, 2048, 3584], P('section', ('node', 'local')), may hold values from -6 to 6
- route_bwd: int32 [8, 2048, 2], P('section', ('node', 'local')), may hold values from 0 to 3, all different within a row; in each aligned block of 64 rows (0 to 63, 64 to 127, ..., all dimensions but the last counted through in order) at most 36 rows name the same one
- weight_bwd: float32 [8, 2048, 2], P('section', ('node', 'local')), may hold values from 0.2 to 1.2
- saved_pre: bfloat16 [8, 4, 1152, 2, 2048], P('section', 'node', None, None, 'local'), may hold values from -6 to 6
- norm_gain: float32 [8, 3584], P('section'), may hold values from 0.5 to 1.5
- w_gate: bfloat16 [8, 4, 3584, 2048], P('section', 'node', None, 'local'), may hold values from -0.09375 to 0.09375
- w_up: bfloat16 [8, 4, 3584, 2048], P('section', 'node', None, 'local'), may hold values from -0.09375 to 0.09375
- w_down: bfloat16 [8, 4, 2048, 3584], P('section', 'node', 'local'), may hold values from -0.125 to 0.125
Outputs:
- act_next: bfloat16 [8, 2048, 3584], P('section', ('node', 'local'))
- grad_prev: bfloat16 [8, 2048, 3584], P('section', ('node', 'local'))
The draws below stay inside these ranges and needn't reach their ends.
Inputs may be any that keep to these rules, and one draw needn't show every extreme that they name: `route_fwd`: each row names 2 different experts. Among the 64 rows of one device no expert is named more than 36 times, and in every draw some device names some expert exactly 36 times. `route_bwd`: each row names 2 different experts. Among the 64 rows of one device no expert is named more than 36 times, and in every draw some device names some expert exactly 36 times.
All inputs are finite; a program needn't handle non-finite values.
Results may differ from the reference program's by a relative error of at most 0.01.
Values may be sent and summed in bfloat16 or wider, within the bound.
No kernel may reach another device: no remote copies, remote signals or barrier semaphores. Data moves between devices by JAX's collectives and lax.ppermute only.
A program may use at most 128 MiB of HBM per device.

```python
import math
import jax
import jax.numpy as jnp
import numpy as np
from jax import lax

D = 3584
HID = 2048
TOPK = 2
TOK_DEV = 64
SECTIONS = 8
EXPERTS = 4
H_DEV = 256
CAP = 36
TOKENS = 2048
ROWS = 1152
N_NODE = 4
N_LOCAL = 8


def shard_levels(key, shape, shards, low, largest):
    def one(position, shards_of):
        draws = jax.random.uniform(jax.random.fold_in(jax.random.fold_in(key, 6), position), (shards_of,), jnp.float32, low / len(shards), largest / len(shards))
        return jnp.repeat(jnp.exp(draws), shape[position] // shards_of).reshape((-1,) + (1,) * (len(shape) - position - 1))

    factor_of = one(*shards[0])
    for cut in shards[1:]:
        factor_of = factor_of * one(*cut)
    return factor_of


def assign_block(own_key, own, number, rows, amount, top, limit, slope):
    sequence = jax.random.permutation(own_key, amount)
    packed, usual = portions_of(amount, rows * top, limit, slope, True), portions_of(amount, rows * top, limit, slope, False)
    places = jnp.arange(amount)

    def named(sizes, offset_by):
        used = int((sizes > 0).sum())
        fixed = max(1, used // 4)
        passed = fixed + (places - fixed + offset_by * (used - fixed)) % max(1, amount - fixed)
        return jnp.zeros((amount,), jnp.int32).at[sequence[jnp.where(places < fixed, places, passed)]].set(jnp.asarray(sizes, jnp.int32))

    sizes = jnp.where(number % 4 == 0, named(packed, number // 4), named(usual, number - number // 4 - 1))
    mixed = jax.random.permutation(jax.random.fold_in(own, 3), amount)
    donor, taker = mixed[0:amount // 2 * 2:2], mixed[1:amount // 2 * 2:2]
    room = jnp.minimum(sizes[donor] - 1, limit - sizes[taker]) // 2
    room = jnp.where((donor == sequence[0]) | (taker == sequence[0]) | (sizes[taker] == 0), 0, jnp.maximum(room, 0))
    passed = jax.random.randint(jax.random.fold_in(own, 4), (amount // 2,), 0, 1 << 20) % (room + 1)
    sizes = sizes.at[donor].add(-passed).at[taker].add(passed)
    items = jnp.searchsorted(jnp.cumsum(sizes), jnp.arange(rows * top), side="right").astype(jnp.int32)
    listing = items.reshape(top, rows).T
    listing = listing[jax.random.permutation(jax.random.fold_in(own, 1), rows)]
    offset_by = jax.random.randint(jax.random.fold_in(own, 2), (rows, 1), 0, top)
    return jnp.take_along_axis(listing, (jnp.arange(top)[None, :] + offset_by) % top, axis=1)


def portions_of(number_of, total, most, lean, full):
    weights = [(1 << 20) // math.isqrt(rank ** lean) + 1 for rank in range(1, number_of + 1)]
    largest = most if full else min(most, max(-(-total // number_of), total * weights[0] // sum(weights)))
    least = 1 if total - largest >= number_of - 1 else 0
    counts, spare = [largest] + [least] * (number_of - 1), total - largest - least * (number_of - 1)
    while spare > 0:
        candidates = [i for i in range(1, number_of) if counts[i] < largest] or [i for i in range(1, number_of) if counts[i] < most]
        mass, budget = sum([weights[i] for i in candidates]), spare
        for i in candidates:
            addition = min(most - counts[i], max(1, budget * weights[i] // mass), spare)
            counts[i] = counts[i] + addition
            spare = spare - addition
    return np.array(counts)


def centred(own_key, shape, deviation, bound, shards=(), held_as=jnp.bfloat16):
    entries = deviation * jax.random.normal(own_key, shape, jnp.float32)
    if shards:
        entries = entries * shard_levels(own_key, shape, shards, -0.22, 0.18)
    return jnp.clip(entries, -bound, bound).astype(held_as)


def setup_inputs(seed: int = 0) -> dict:
    key_list = jax.random.split(jax.random.key(seed), 13)
    x_fwd = centred(key_list[0], (SECTIONS, TOKENS, D), 1.0, 6.0, ((0, 8), (1, 32)))
    route_fwd_keys = jax.random.split(jax.random.fold_in(key_list[1], 1), SECTIONS * TOKENS // TOK_DEV)
    route_fwd_turns = jax.random.permutation(jax.random.fold_in(key_list[1], 3), SECTIONS * TOKENS // TOK_DEV)
    route_fwd = jax.vmap(lambda own, number: assign_block(jax.random.fold_in(key_list[1], 2), own, number, TOK_DEV, EXPERTS, TOPK, CAP, 2))(route_fwd_keys, route_fwd_turns).reshape((SECTIONS, TOKENS, TOPK))
    weight_fwd = jnp.clip(0.2 + 1 * jax.random.uniform(key_list[2], (SECTIONS, TOKENS, TOPK), jnp.float32) ** shard_levels(key_list[2], (SECTIONS, TOKENS, TOPK), ((0, 8), (1, 32)), -0.2, 0.2), 0.2, 1.2)
    x_bwd = centred(key_list[3], (SECTIONS, TOKENS, D), 1.0, 6.0, ((0, 8), (1, 32)))
    grad_out = centred(key_list[4], (SECTIONS, TOKENS, D), 1.0, 6.0, ((0, 8), (1, 32)))
    route_bwd_keys = jax.random.split(jax.random.fold_in(key_list[5], 1), SECTIONS * TOKENS // TOK_DEV)
    route_bwd_turns = jax.random.permutation(jax.random.fold_in(key_list[5], 3), SECTIONS * TOKENS // TOK_DEV)
    route_bwd = jax.vmap(lambda own, number: assign_block(jax.random.fold_in(key_list[5], 2), own, number, TOK_DEV, EXPERTS, TOPK, CAP, 2))(route_bwd_keys, route_bwd_turns).reshape((SECTIONS, TOKENS, TOPK))
    weight_bwd = jnp.clip(0.2 + 1 * jax.random.uniform(key_list[6], (SECTIONS, TOKENS, TOPK), jnp.float32) ** shard_levels(key_list[6], (SECTIONS, TOKENS, TOPK), ((0, 8), (1, 32)), -0.2, 0.2), 0.2, 1.2)
    saved_pre = centred(key_list[7], (SECTIONS, EXPERTS, ROWS, 2, HID), 1.0, 6.0, ((0, 8), (1, 4), (4, 8)))
    norm_gain = jnp.clip(0.5 + 1.0 * jax.random.uniform(key_list[8], (SECTIONS, D), jnp.float32) ** shard_levels(key_list[8], (SECTIONS, D), ((0, 8),), -0.2, 0.2), 0.5, 1.5)
    w_gate = centred(key_list[9], (SECTIONS, EXPERTS, D, HID), D ** -0.5, 0.09375, ((0, 8), (1, 4), (3, 8)))
    w_up = centred(key_list[10], (SECTIONS, EXPERTS, D, HID), D ** -0.5, 0.09375, ((0, 8), (1, 4), (3, 8)))
    w_down = centred(key_list[11], (SECTIONS, EXPERTS, HID, D), HID ** -0.5, 0.125, ((0, 8), (1, 4), (2, 8)))
    return dict(x_fwd=x_fwd, route_fwd=route_fwd, weight_fwd=weight_fwd, x_bwd=x_bwd, grad_out=grad_out, route_bwd=route_bwd, weight_bwd=weight_bwd, saved_pre=saved_pre, norm_gain=norm_gain, w_gate=w_gate, w_up=w_up, w_down=w_down)


EPSILON = 1e-06

def rms_scale(values):
    return lax.rsqrt(lax.optimization_barrier(jnp.mean(values * values, axis=-1, keepdims=True)) + EPSILON)

def slot_rows(route):
    blocks = N_NODE * N_LOCAL
    grouped = route.reshape(blocks, TOK_DEV, TOPK)
    choose = (grouped[:, :, :, None] == jnp.arange(EXPERTS, dtype=jnp.int32)[None, None, None, :]).astype(jnp.int32)
    per_token = lax.optimization_barrier(jnp.sum(choose, axis=2))
    earlier = jnp.cumsum(per_token, axis=1) - per_token
    slot = lax.optimization_barrier(jnp.sum(choose * earlier[:, :, None, :], axis=3))
    block_id = jnp.arange(blocks, dtype=jnp.int32)[:, None, None]
    source = block_id % N_LOCAL * N_NODE + block_id // N_LOCAL
    return (grouped * ROWS + source * CAP + slot).astype(jnp.int32).reshape(TOKENS, TOPK)

def place(source_rows, target):
    empty = jnp.zeros((EXPERTS * ROWS, D), jnp.bfloat16)
    return empty.at[target].set(source_rows).reshape(EXPERTS, ROWS, D)

def shard_sum(left_parts, right_parts):

    def add_part(total, pair):
        part = jnp.dot(pair[0], pair[1], preferred_element_type=jnp.float32).astype(jnp.bfloat16)
        part = lax.optimization_barrier(part)
        return (total + part.astype(jnp.float32), None)
    total, unused = lax.scan(add_part, jnp.zeros((ROWS, D), jnp.float32), (left_parts, right_parts))
    return total.astype(jnp.bfloat16)

def expert_forward(group):
    block, gate_w, up_w, down_w = group
    gate = jnp.dot(block, gate_w, preferred_element_type=jnp.float32)
    upper = jnp.dot(block, up_w, preferred_element_type=jnp.float32)
    hidden = (jax.nn.silu(gate) * upper).astype(jnp.bfloat16)
    left_parts = hidden.reshape(ROWS, N_LOCAL, H_DEV).transpose(1, 0, 2)
    return shard_sum(left_parts, down_w.reshape(N_LOCAL, H_DEV, D))

def expert_backward(group):
    block, saved, gate_w, up_w, down_w = group
    hidden_grad = jnp.dot(block, down_w.T, preferred_element_type=jnp.float32)
    gate = saved[:, 0, :].astype(jnp.float32)
    upper = saved[:, 1, :].astype(jnp.float32)
    sigma = jax.nn.sigmoid(gate)
    grad_gate = (hidden_grad * upper * sigma * (1.0 + gate * (1.0 - sigma))).astype(jnp.bfloat16)
    grad_upper = (hidden_grad * gate * sigma).astype(jnp.bfloat16)
    left_parts = jnp.concatenate([grad_gate.reshape(ROWS, N_LOCAL, H_DEV), grad_upper.reshape(ROWS, N_LOCAL, H_DEV)], axis=2).transpose(1, 0, 2)
    right_parts = jnp.concatenate([gate_w.T.reshape(N_LOCAL, H_DEV, D), up_w.T.reshape(N_LOCAL, H_DEV, D)], axis=1)
    return shard_sum(left_parts, right_parts)

def section_step(inputs):
    x_first, route_first, weight_first, x_second, upstream, route_second, weight_second, saved, gain, gate_w, up_w, down_w = inputs
    first = x_first.astype(jnp.float32)
    normed = (first * rms_scale(first) * gain).astype(jnp.bfloat16)
    rows_first = slot_rows(route_first)
    dispatched = place(jnp.repeat(normed, TOPK, axis=0), rows_first.reshape(-1))
    expert_out = lax.map(expert_forward, (dispatched, gate_w, up_w, down_w))
    picked = jnp.take(expert_out.reshape(EXPERTS * ROWS, D), rows_first.reshape(-1), axis=0)
    picked = picked.reshape(TOKENS, TOPK, D).astype(jnp.float32)
    layer_out = (first + lax.optimization_barrier(jnp.sum(weight_first[:, :, None] * picked, axis=1))).astype(jnp.bfloat16)
    second = x_second.astype(jnp.float32)
    scale = rms_scale(second)
    scaled = (weight_second[:, :, None] * upstream[:, None, :].astype(jnp.float32)).astype(jnp.bfloat16)
    rows_second = slot_rows(route_second)
    dispatched_back = place(scaled.reshape(TOKENS * TOPK, D), rows_second.reshape(-1))
    expert_grad = lax.map(expert_backward, (dispatched_back, saved, gate_w, up_w, down_w))
    picked_back = jnp.take(expert_grad.reshape(EXPERTS * ROWS, D), rows_second.reshape(-1), axis=0)
    normed_grad = lax.optimization_barrier(jnp.sum(picked_back.reshape(TOKENS, TOPK, D).astype(jnp.float32), axis=1))
    along = gain * normed_grad
    input_grad = upstream.astype(jnp.float32) + scale * along - second * (scale * scale * scale) * lax.optimization_barrier(jnp.mean(along * second, axis=-1, keepdims=True))
    return (layer_out, input_grad.astype(jnp.bfloat16))

def reference(x_fwd, route_fwd, weight_fwd, x_bwd, grad_out, route_bwd, weight_bwd, saved_pre, norm_gain, w_gate, w_up, w_down):
    layer_out, input_grad = lax.map(section_step, (x_fwd, route_fwd, weight_fwd, x_bwd, grad_out, route_bwd, weight_bwd, saved_pre, norm_gain, w_gate, w_up, w_down))
    return (jnp.roll(layer_out, 1, axis=0), jnp.roll(input_grad, -1, axis=0))
```

```python
import jax
import jax.numpy as jnp
from jax import lax
from jax.sharding import PartitionSpec as P

EPSILON = 1e-06
Y_SIZE = 4
PARTS = 4
META = 128
BF16 = jnp.bfloat16
F32 = jnp.float32
FEATURES_LAST = (((1,), (1,)), ((), ()))
ROWS_FIRST = (((0,), (0,)), ((), ()))
Z_ORDER = (0, -1, 1, -2, 2, -3, 3, 4)


def shift_y(value, by):
    count = lax.axis_size("local")
    pairs = [(i, i // Y_SIZE * Y_SIZE + (i % Y_SIZE + by) % Y_SIZE) for i in range(count)]
    return lax.ppermute(value, "local", pairs)


def shift_z(value, by):
    nodes = lax.axis_size("node")
    locals_ = lax.axis_size("local")
    depth = nodes * (locals_ // Y_SIZE)
    pairs = []
    for node in range(nodes):
        for place in range(locals_):
            z = (place // Y_SIZE) * nodes + node
            to = (z + by) % depth
            pairs.append(
                (node * locals_ + place, (to % nodes) * locals_ + to // nodes * Y_SIZE + place % Y_SIZE)
            )
    return lax.ppermute(value, ("node", "local"), pairs)


def shift_section(value, by):
    size = lax.axis_size("section")
    return lax.ppermute(value, "section", [(i, (i + by) % size) for i in range(size)])


def rms_scale(values):
    return lax.rsqrt(jnp.mean(values * values, axis=-1, keepdims=True) + EPSILON)


def gather_z(block, flip):
    got = {0: block}
    for step in range(1, 5 if not flip else 4):
        got[-step] = shift_z(got[-(step - 1)], 1)
    for step in range(1, 4 if not flip else 5):
        got[step] = shift_z(got[step - 1], -1)
    got[4] = got[4] if 4 in got else got[-4]
    return [got[i] for i in Z_ORDER]


def gather_y(block, flip):
    before = shift_y(block, 1)
    after = shift_y(block, -1)
    far = shift_y(after, -1) if flip else shift_y(before, 1)
    return {0: block, -1: before, 1: after, 2: far}


def scatter_y(term, flip):
    side = -1 if flip else 1
    far = shift_y(term(2).astype(BF16), side)
    through = shift_y((term(side) + far.astype(F32)).astype(BF16), side)
    direct = shift_y(term(-side).astype(BF16), -side)
    return term(0) + through.astype(F32) + direct.astype(F32)


def scatter_z(term, flip):
    side = -1 if flip else 1
    long = shift_z(term(4).astype(BF16), side)
    for step in (3, 2, 1):
        long = shift_z((term(side * step) + long.astype(F32)).astype(BF16), side)
    short = shift_z(term(-side * 3).astype(BF16), -side)
    for step in (2, 1):
        short = shift_z((term(-side * step) + short.astype(F32)).astype(BF16), -side)
    return term(0) + long.astype(F32) + short.astype(F32)


def slots_of(route, experts):
    named = route[:, :, None] == jnp.arange(experts, dtype=jnp.int32)[None, None, :]
    chosen = jnp.any(named, axis=1)
    rows = route.shape[0]
    earlier = lax.broadcasted_iota(jnp.int32, (rows, rows), 1) < lax.broadcasted_iota(
        jnp.int32, (rows, rows), 0
    )
    before = jnp.dot(earlier.astype(BF16), chosen.astype(BF16), preferred_element_type=F32)
    return named, jnp.where(chosen, before, -1.0)


def split_three(value):
    first = value.astype(BF16)
    rest = value - first.astype(F32)
    second = rest.astype(BF16)
    third = (rest - second.astype(F32)).astype(BF16)
    return [first, second, third]


def describe(route, weight, experts):
    named, slot = slots_of(route, experts)
    spread = jnp.sum(jnp.where(named, weight[:, :, None], 0.0), axis=1)
    return [slot.astype(BF16)] + split_three(spread)


def local(
    x_fwd,
    route_fwd,
    weight_fwd,
    x_bwd,
    grad_out,
    route_bwd,
    weight_bwd,
    saved_pre,
    norm_gain,
    w_gate,
    w_up,
    w_down,
):
    experts = lax.axis_size("node")
    halves = lax.axis_size("local") // Y_SIZE
    depth = experts * halves
    tokens, width = x_fwd.shape[1:]
    units = w_gate.shape[3]
    slot_total = saved_pre.shape[2]
    capacity = slot_total // (depth * Y_SIZE)
    group = depth * capacity
    part = width // PARTS
    expert = lax.axis_index("node")
    place = lax.axis_index("local")
    my_y = place % Y_SIZE
    my_z = place // Y_SIZE * experts + expert

    both_w = jnp.concatenate([w_gate[0, 0], w_up[0, 0]], axis=1)
    down_w = w_down[0, 0]
    gain = norm_gain[0]
    upstream = grad_out[0]

    def columns(value, c):
        return value[:, c * part : (c + 1) * part]

    pieces = describe(route_fwd[0], weight_fwd[0], experts) + describe(
        route_bwd[0], weight_bwd[0], experts
    )
    meta = jnp.concatenate(pieces, axis=1)
    meta = jnp.pad(meta, ((0, 0), (0, META - meta.shape[1])))

    gathered = [
        gather_z(
            jnp.concatenate([columns(upstream, 0), meta], axis=1) if c == 0 else columns(upstream, c),
            c % 2 == 1,
        )
        for c in range(PARTS)
    ]
    x_first = x_fwd[0].astype(F32)
    normed = (x_first * rms_scale(x_first) * gain).astype(BF16)
    gathered_first = [gather_z(columns(normed, c), c % 2 == 1) for c in range(PARTS)]

    stacked = [jnp.concatenate(blocks, axis=0) for blocks in gathered]
    metas = stacked[0][:, part:]
    mine = lax.broadcasted_iota(jnp.int32, (1, experts), 1) == expert

    def pick(values, index):
        cut = values[:, index * experts : (index + 1) * experts].astype(F32)
        return jnp.sum(jnp.where(mine, cut, 0.0), axis=1, keepdims=True)

    z_of = jnp.concatenate(
        [jnp.full((tokens, 1), (my_z + i + depth) % depth, jnp.int32) for i in Z_ORDER], axis=0
    )

    def table(index):
        slot = pick(metas, index).astype(jnp.int32)
        target = jnp.where(slot >= 0, z_of * capacity + slot, -1)
        return (
            target == lax.broadcasted_iota(jnp.int32, (depth * tokens, group), 1)
        ).astype(BF16)

    table_first = table(0)
    table_second = table(4)

    def choose(chosen, values):
        return lax.dot_general(chosen, values, ROWS_FIRST, preferred_element_type=F32)

    def weights_of(picked, index):
        return pick(picked, index + 1) + pick(picked, index + 2) + pick(picked, index + 3)

    opening = choose(table_second, stacked[0])
    slot_weight_second = weights_of(opening[:, part:], 4)
    slot_weight_first = weights_of(choose(table_first, metas), 0)

    arrived_second = []
    for c in range(PARTS):
        rows = opening[:, :part] if c == 0 else choose(table_second, stacked[c])
        arrived_second.append(gather_y((rows * slot_weight_second).astype(BF16), c % 2 == 1))
    arrived_first = []
    for c in range(PARTS):
        rows = choose(table_first, jnp.concatenate(gathered_first[c], axis=0))
        arrived_first.append(gather_y(rows.astype(BF16), c % 2 == 1))

    saved = saved_pre[0, 0].reshape(halves, Y_SIZE, experts * capacity, 2, units)
    pre_grads = {}
    for r in (2, 1, -1, 0):
        hidden_grad = sum(
            lax.dot_general(
                arrived_second[c][r], columns(down_w, c), FEATURES_LAST, preferred_element_type=F32
            )
            for c in range(PARTS)
        )
        stored = lax.dynamic_index_in_dim(
            saved, (my_y + r + Y_SIZE) % Y_SIZE, 1, keepdims=False
        ).reshape(group, 2, units)
        gate = stored[:, 0, :].astype(F32)
        upper = stored[:, 1, :].astype(F32)
        sigma = jax.nn.sigmoid(gate)
        grad_gate = hidden_grad * upper * sigma * (1.0 + gate * (1.0 - sigma))
        grad_upper = hidden_grad * gate * sigma
        pre_grads[r] = jnp.concatenate([grad_gate, grad_upper], axis=1).astype(BF16)

    hidden = {}
    for r in (2, 1, -1, 0):
        both = sum(
            jnp.dot(
                arrived_first[c][r],
                both_w[c * part : (c + 1) * part],
                preferred_element_type=F32,
            )
            for c in range(PARTS)
        )
        hidden[r] = (jax.nn.silu(both[:, :units]) * both[:, units:]).astype(BF16)

    def give_back(chosen, rows, flip):
        rows = rows.astype(BF16)

        def term(i):
            at = Z_ORDER.index(i) * tokens
            return jnp.dot(chosen[at : at + tokens], rows, preferred_element_type=F32)

        return scatter_z(term, flip)

    normed_grad = []
    for c in range(PARTS):
        rows = scatter_y(
            lambda r: lax.dot_general(
                pre_grads[r],
                both_w[c * part : (c + 1) * part],
                FEATURES_LAST,
                preferred_element_type=F32,
            ),
            c % 2 == 1,
        )
        normed_grad.append(give_back(table_second, rows, c % 2 == 1))

    x_second = x_bwd[0].astype(F32)
    scale = rms_scale(x_second)
    along = gain * jnp.concatenate(normed_grad, axis=1)
    input_grad = (
        upstream.astype(F32)
        + scale * along
        - x_second * (scale * scale * scale) * jnp.mean(along * x_second, axis=-1, keepdims=True)
    )
    grad_prev = shift_section(input_grad.astype(BF16), -1)

    act_next = []
    for c in range(PARTS):
        rows = scatter_y(
            lambda r: jnp.dot(hidden[r], columns(down_w, c), preferred_element_type=F32),
            c % 2 == 1,
        )
        added = give_back(table_first, rows * slot_weight_first, c % 2 == 1)
        act_next.append(shift_section((columns(x_first, c) + added).astype(BF16), 1))
    return (jnp.concatenate(act_next, axis=1)[None], grad_prev[None])


def solution(mesh):
    tokens = P("section", ("node", "local"), None)
    in_specs = (
        tokens,
        tokens,
        tokens,
        tokens,
        tokens,
        tokens,
        tokens,
        P("section", "node", None, None, "local"),
        P("section", None),
        P("section", "node", None, "local"),
        P("section", "node", None, "local"),
        P("section", "node", "local", None),
    )
    return jax.shard_map(
        local, mesh=mesh, in_specs=in_specs, out_specs=(tokens, tokens), check_vma=False
    )
```

```python
import functools

import jax
import jax.numpy as jnp
from jax import lax
from jax.experimental import pallas as pl
from jax.experimental.pallas import tpu as pltpu
from jax.sharding import PartitionSpec as P

EPSILON = 1e-06
Y_SIZE = 4
LANES = 128
VMEM_BYTES = 24 * 1024 * 1024
CUT_SECOND = (4, 10, 14)
CUT_FIRST = (14, 14)
CUT_END = (7, 7)
CUT_BACK = (14, 14)
CUT_LAST = (8, 8, 6, 6)
BF16 = jnp.bfloat16
F32 = jnp.float32
FEATURES_LAST = (((1,), (1,)), ((), ()))
Z_ORDER = (0, 4, -1, 3, 1, -3, -2, 2)


def shift_y(value, by):
    count = lax.axis_size("local")
    pairs = [(i, i // Y_SIZE * Y_SIZE + (i % Y_SIZE + by) % Y_SIZE) for i in range(count)]
    return lax.ppermute(value, "local", pairs)


def shift_z(value, by):
    nodes = lax.axis_size("node")
    locals_ = lax.axis_size("local")
    depth = nodes * (locals_ // Y_SIZE)
    pairs = []
    for node in range(nodes):
        for place in range(locals_):
            z = (place // Y_SIZE) * nodes + node
            to = (z + by) % depth
            pairs.append(
                (node * locals_ + place, (to % nodes) * locals_ + to // nodes * Y_SIZE + place % Y_SIZE)
            )
    return lax.ppermute(value, ("node", "local"), pairs)


def shift_section(value, by):
    size = lax.axis_size("section")
    return lax.ppermute(value, "section", [(i, (i + by) % size) for i in range(size)])


def hold(value, *marks):
    marks = [mark for mark in marks if mark is not None]
    return lax.optimization_barrier((value, marks))[0] if marks else value


def back(items, count):
    return items[-count] if len(items) >= count else None


def rms_scale(values):
    return lax.rsqrt(jnp.mean(values * values, axis=-1, keepdims=True) + EPSILON)


def cut(width, shares):
    units = width // LANES
    total = sum(shares)
    edges = [round(units * sum(shares[:i]) / total) * LANES for i in range(len(shares) + 1)]
    return list(zip(edges[:-1], edges[1:]))


def tile_of(width):
    units = width // LANES
    return LANES * max(i for i in range(1, 8) if units % i == 0)


def params():
    return pltpu.CompilerParams(vmem_limit_bytes=VMEM_BYTES)


def cost(flops, moved):
    return pl.CostEstimate(flops=flops, bytes_accessed=moved, transcendentals=0)


def opening_kernel(edges, route_f, weight_f, route_b, weight_b, rows, *outs):
    count = rows.shape[0]
    lane = lax.broadcasted_iota(jnp.int32, (count, LANES), 1)
    earlier = (
        lax.broadcasted_iota(jnp.int32, (count, count), 1)
        < lax.broadcasted_iota(jnp.int32, (count, count), 0)
    ).astype(BF16)
    kind = lane // 4
    meta = jnp.zeros((count, LANES), F32)
    for start, route, weight in ((0, route_f, weight_f), (4, route_b, weight_b)):
        first = route[:, 0:1] == lane % 4
        second = route[:, 1:2] == lane % 4
        chosen = jnp.where(first, 1.0, jnp.where(second, 1.0, 0.0))
        before = jnp.dot(earlier, chosen.astype(BF16), preferred_element_type=F32)
        value = jnp.where(first, weight[:, 0:1], jnp.where(second, weight[:, 1:2], 0.0))
        high = value.astype(BF16).astype(F32)
        middle = (value - high).astype(BF16).astype(F32)
        low = value - high - middle
        meta = jnp.where(kind == start, jnp.where(chosen > 0.0, before, -1.0), meta)
        meta = jnp.where(kind == start + 1, high, meta)
        meta = jnp.where(kind == start + 2, middle, meta)
        meta = jnp.where(kind == start + 3, low, meta)
    for i, ((low_edge, high_edge), out) in enumerate(zip(edges, outs)):
        span = high_edge - low_edge
        out[:, :span] = rows[:, low_edge:high_edge]
        if i == 0:
            out[:, span:] = meta.astype(BF16)


def opening(edges, route_f, weight_f, route_b, weight_b, rows):
    count = rows.shape[0]
    shapes = [
        jax.ShapeDtypeStruct((count, high - low + (LANES if i == 0 else 0)), BF16)
        for i, (low, high) in enumerate(edges)
    ]
    return pl.pallas_call(
        functools.partial(opening_kernel, edges),
        out_shape=shapes,
        compiler_params=params(),
        cost_estimate=cost(0, 4 * rows.size),
    )(route_f, weight_f, route_b, weight_b, rows)


def norm_kernel(edges, rows, gain, *outs):
    values = rows[...].astype(F32)
    normed = (values * rms_scale(values) * gain[...]).astype(BF16)
    for (low, high), out in zip(edges, outs):
        out[...] = normed[:, low:high]


def norm(edges, rows, gain):
    return pl.pallas_call(
        functools.partial(norm_kernel, edges),
        out_shape=[
            jax.ShapeDtypeStruct((rows.shape[0], high - low), BF16) for low, high in edges
        ],
        compiler_params=params(),
        cost_estimate=cost(8 * rows.size, 4 * rows.size),
    )(rows, gain)


def tables_kernel(capacity, slots, expert, z_of, *refs):
    blocks, outs = refs[:8], refs[8:]
    metas = jnp.concatenate([ref[...].astype(F32) for ref in blocks], axis=0)
    count = metas.shape[0]
    lane = lax.broadcasted_iota(jnp.int32, metas.shape, 1)
    mine = lane % 4 == expert[...]
    kind = lane // 4
    padded = outs[0].shape[0] // LANES * LANES + (LANES if outs[0].shape[0] % LANES else 0)
    places = lax.broadcasted_iota(jnp.int32, (count, padded), 1)
    for i, start in enumerate((0, 4)):
        slot = jnp.sum(jnp.where(mine & (kind == start), metas, 0.0), axis=1, keepdims=True)
        high = mine & (kind > start) & (kind < start + 4)
        weight = jnp.sum(jnp.where(high, metas, 0.0), axis=1, keepdims=True)
        target = jnp.where(slot >= 0.0, z_of[...] * capacity + slot.astype(jnp.int32), -1)
        down = jnp.where(target == places, 1.0, 0.0)
        across, down_out, weight_out = outs[3 * i : 3 * i + 3]
        down_out[...] = down[:, :slots].astype(BF16)
        across[...] = down.T[:slots].astype(BF16)
        weight_out[...] = jnp.sum((down * weight).T, axis=1, keepdims=True)[:slots]


def tables(expert, z_of, blocks, row, column, capacity):
    count = z_of.shape[0]
    slots = capacity * len(blocks)
    step = count // len(blocks)
    one = [
        jax.ShapeDtypeStruct((slots, count), BF16),
        jax.ShapeDtypeStruct((count, slots), BF16),
        jax.ShapeDtypeStruct((slots, 1), F32),
    ]
    whole = lambda shape: pl.BlockSpec(shape, lambda i: (0, 0))
    return pl.pallas_call(
        functools.partial(tables_kernel, capacity, slots),
        grid=(1,),
        out_shape=one * 2,
        in_specs=[whole((1, LANES)), whole((count, 1))]
        + [pl.BlockSpec((step, LANES), lambda i: (row, column))] * len(blocks),
        out_specs=[whole(item.shape) for item in one * 2],
        compiler_params=params(),
        cost_estimate=cost(0, 8 * slots * count),
    )(expert, z_of, *blocks)


def select_kernel(table, scale, *refs):
    blocks, out = refs[:-1], refs[-1]
    values = jnp.concatenate([ref[...] for ref in blocks], axis=0)
    total = jnp.dot(table[...], values, preferred_element_type=F32)
    out[...] = (total * scale[...]).astype(BF16)


def select(table, scale, blocks, width, row=0, column=0):
    rows, tokens = table.shape
    tile = tile_of(width)
    step = tokens // len(blocks)
    return pl.pallas_call(
        select_kernel,
        grid=(width // tile,),
        out_shape=jax.ShapeDtypeStruct((rows, width), BF16),
        in_specs=[
            pl.BlockSpec((rows, tokens), lambda i: (0, 0)),
            pl.BlockSpec((rows, 1), lambda i: (0, 0)),
        ]
        + [pl.BlockSpec((step, tile), lambda i: (row, i + column // tile))] * len(blocks),
        out_specs=pl.BlockSpec((rows, tile), lambda i: (0, i)),
        compiler_params=params(),
        cost_estimate=cost(2 * rows * tokens * width, 2 * (rows + tokens) * width),
    )(table, scale, *blocks)


def spread_kernel(table, scale, rows, *outs):
    values = (rows[...] * scale[...]).astype(BF16)
    total = jnp.dot(table[...], values, preferred_element_type=F32).astype(BF16)
    step = table.shape[0] // len(outs)
    for i, ref in enumerate(outs):
        ref[...] = total[i * step : (i + 1) * step]


def spread(table, scale, rows, count):
    tokens, slots = table.shape
    width = rows.shape[1]
    tile = tile_of(width)
    return pl.pallas_call(
        spread_kernel,
        grid=(width // tile,),
        out_shape=[jax.ShapeDtypeStruct((tokens // count, width), BF16)] * count,
        in_specs=[
            pl.BlockSpec((tokens, slots), lambda i: (0, 0)),
            pl.BlockSpec((slots, 1), lambda i: (0, 0)),
            pl.BlockSpec((slots, tile), lambda i: (0, i)),
        ],
        out_specs=[pl.BlockSpec((tokens // count, tile), lambda i: (0, i))] * count,
        compiler_params=params(),
        cost_estimate=cost(2 * slots * tokens * width, (4 * slots + 2 * tokens) * width),
    )(table, scale, rows)


def local(
    x_fwd,
    route_fwd,
    weight_fwd,
    x_bwd,
    grad_out,
    route_bwd,
    weight_bwd,
    saved_pre,
    norm_gain,
    w_gate,
    w_up,
    w_down,
):
    experts = lax.axis_size("node")
    halves = lax.axis_size("local") // Y_SIZE
    depth = experts * halves
    tokens, width = x_fwd.shape[1:]
    units = w_gate.shape[3]
    capacity = saved_pre.shape[2] // (depth * Y_SIZE)
    group = depth * capacity
    expert = lax.axis_index("node")
    place = lax.axis_index("local")
    my_y = place % Y_SIZE
    my_z = place // Y_SIZE * experts + expert
    gain = norm_gain[0]
    upstream = grad_out[0]

    def columns(value, edge):
        return value[:, edge[0] : edge[1]]

    cuts_second = cut(width, CUT_SECOND)
    cuts_first = cut(width, CUT_FIRST)
    cuts_back = cut(width, CUT_BACK)
    cuts_last = cut(width, CUT_LAST)
    blocks = opening(
        cuts_second, route_fwd[0], weight_fwd[0], route_bwd[0], weight_bwd[0], upstream
    )
    expert_row = jnp.full((1, LANES), expert, jnp.int32)
    z_of = jnp.concatenate(
        [jnp.full((tokens, 1), (my_z + i + depth) % depth, jnp.int32) for i in Z_ORDER], axis=0
    )
    ones = jnp.ones((group, 1), F32)

    firsts, thirds, starts, turns = [], [], [], []

    def open_z(block):
        block = hold(block, back(firsts, 1), back(starts, 2))
        got = {0: block, -1: shift_z(block, 1), 1: shift_z(block, -1)}
        firsts.append((got[-1], got[1]))
        return got

    def close_z(got, flip, *marks):
        got[-1], got[1] = hold((got[-1], got[1]), back(thirds, 1))
        for step in range(2, 5):
            if step == 3:
                got[-2], got[2] = hold((got[-2], got[2]), *marks)
            if step == 4:
                got[-3], got[3] = hold((got[-3], got[3]), firsts[-1])
            if step < 4 or not flip:
                got[-step] = shift_z(got[1 - step], 1)
            if step < 4 or flip:
                got[step] = shift_z(got[step - 1], -1)
        thirds.append((got[-3], got[3]))
        got[4] = got[4] if flip else got[-4]
        return [got[i] for i in Z_ORDER]

    def gather_y(block, *marks):
        block = hold(block, back(starts, 2), back(turns, 2), *marks)
        before = shift_y(block, 1)
        after = shift_y(block, -1)
        starts.append((before, after))
        return block, before, after

    def finish_y(parts, flip, *marks):
        block, before, after = parts
        first = hold(after if flip else before, *marks)
        far = shift_y(first, -1 if flip else 1)
        turns.append(far)
        return {0: block, -1: before, 1: after, 2: far}

    block = blocks[0]
    direct = [block if i == 0 else shift_z(block, -i) for i in Z_ORDER]
    firsts.append((direct[2], direct[4]))
    x_first = x_fwd[0]
    blocks += norm(cuts_first, hold(x_first, direct[2]), gain.reshape(1, width))
    across_first, down_first, weight_first, across_second, down_second, weight_second = tables(
        expert_row, z_of, direct, 0, cuts_second[0][1] // LANES, capacity
    )

    count_second = len(cuts_second)
    arrived, opened = [], None
    for c, (low, high) in enumerate(cuts_second + cuts_first[:1]):
        flip = c % 2 == 1
        upcoming = open_z(blocks[c + 1])
        parts = close_z(opened, flip, starts[0] if c == 1 else None) if c else direct
        opened = upcoming
        if c < count_second:
            rows = select(across_second, weight_second, parts, high - low)
        else:
            rows = select(across_first, ones, parts, high - low)
        parts = gather_y(rows, None if c else firsts[-1])
        arrived.append(finish_y(parts, flip))
    parts_last = close_z(opened, count_second % 2 == 0)

    gate_w, up_w, down_w, stored_all = hold(
        (w_gate[0, 0], w_up[0, 0], w_down[0, 0], saved_pre[0, 0]), starts[1]
    )
    both_w = jnp.concatenate([gate_w, up_w], axis=1)
    saved = stored_all.reshape(halves, Y_SIZE, experts * capacity, 2, units)
    pre_grads = {}
    for r in (2, 1, -1, 0):
        hidden_grad = sum(
            lax.dot_general(
                parts[r], columns(down_w, edge), FEATURES_LAST, preferred_element_type=F32
            )
            for parts, edge in zip(arrived, cuts_second)
        )
        stored = lax.dynamic_index_in_dim(
            saved, (my_y + r + Y_SIZE) % Y_SIZE, 1, keepdims=False
        ).reshape(group, 2, units)
        gate = stored[:, 0, :].astype(F32)
        upper = stored[:, 1, :].astype(F32)
        sigma = jax.nn.sigmoid(gate)
        grad_gate = hidden_grad * upper * sigma * (1.0 + gate * (1.0 - sigma))
        grad_upper = hidden_grad * gate * sigma
        pre_grads[r] = jnp.concatenate([grad_gate, grad_upper], axis=1).astype(BF16)

    def second_term(edge, r):
        return lax.dot_general(
            pre_grads[r], both_w[edge[0] : edge[1]], FEATURES_LAST, preferred_element_type=F32
        )

    def first_term(edge, r):
        return jnp.dot(hidden[r], columns(down_w, edge), preferred_element_type=F32)

    def start_back(term, edge, side, *marks):
        far, straight = hold((term(edge, 2).astype(BF16), term(edge, -side).astype(BF16)), *marks)
        return shift_y(far, side), shift_y(straight, -side)

    def through_back(term, edge, side, far, straight):
        return shift_y((term(edge, side) + far.astype(F32)).astype(BF16), side)

    def end_back(term, edge, side, far, straight, through):
        return term(edge, 0) + through.astype(F32) + straight.astype(F32)

    def scatter_z(parts, flip, *waits):
        parts = dict(zip(Z_ORDER, parts))
        side = 1 if flip else -1
        long, short = parts[4], parts[-side * 3]
        marks = []
        for step in (3, 2, 1, 0):
            if 3 - step < len(waits):
                long, short = hold((long, short), *waits[3 - step])
            long = shift_z(long, side)
            if step < 3:
                short = shift_z(short, -side)
            marks.append((long, short))
            if step:
                long = (parts[side * step].astype(F32) + long.astype(F32)).astype(BF16)
            if 0 < step < 3:
                short = (parts[-side * step].astype(F32) + short.astype(F32)).astype(BF16)
        return parts[0].astype(F32) + long.astype(F32) + short.astype(F32), marks

    ways = (1, -1, 1, -1)
    begun = [start_back(second_term, *item) for item in zip(cuts_back, ways)]
    turned = [through_back(second_term, *item, *got) for *item, got in zip(cuts_back, ways, begun)]
    rows = [
        end_back(second_term, *item, *got, through)
        for *item, got, through in zip(cuts_back, ways, begun, turned)
    ]
    edges_first = cuts_first[:1] + cut(width - cuts_first[1][0], CUT_END)
    edges_first[1:] = [(low + cuts_first[1][0], high + cuts_first[1][0]) for low, high in edges_first[1:]]
    pending = []
    for i, (low, high) in enumerate(edges_first[1:]):
        rows_first = select(across_first, ones, parts_last, high - low, 0, low - cuts_first[1][0])
        rows_first = hold(rows_first, begun[i])
        pending.append((rows_first, shift_y(rows_first, 1), shift_y(rows_first, -1)))

    arrived.append(finish_y(pending[0], False))
    arrived.append(finish_y(pending[1], True))
    hidden = {}
    for r in (2, 1, -1, 0):
        both = sum(
            jnp.dot(parts[r], both_w[edge[0] : edge[1]], preferred_element_type=F32)
            for parts, edge in zip(arrived[count_second:], edges_first)
        )
        hidden[r] = (jax.nn.silu(both[:, :units]) * both[:, units:]).astype(BF16)

    opened = [
        start_back(first_term, edge, side, turned) for edge, side in zip(cuts_last[:2], ways)
    ]
    parts = spread(down_second, ones, jnp.concatenate(rows, axis=1), depth)
    normed_grad, ring = scatter_z(parts, False, [], [], [opened])
    opened += [
        start_back(first_term, edge, side, ring[0]) for edge, side in zip(cuts_last[2:], ways)
    ]

    x_second = x_bwd[0].astype(F32)
    scale = rms_scale(x_second)
    along = gain * normed_grad
    input_grad = (
        upstream.astype(F32)
        + scale * along
        - x_second * (scale * scale * scale) * jnp.mean(along * x_second, axis=-1, keepdims=True)
    ).astype(BF16)
    grad_prev = shift_section(input_grad, -1)

    act_next = []
    turned = [through_back(first_term, *item, *got) for *item, got in zip(cuts_last, ways, opened)]
    rows = [
        end_back(first_term, *item, *got, through)
        for *item, got, through in zip(cuts_last, ways, opened, turned)
    ]
    for step in range(2):
        pair = jnp.concatenate(rows[2 * step : 2 * step + 2], axis=1)
        edge = (cuts_last[2 * step][0], cuts_last[2 * step + 1][1])
        added, _ = scatter_z(spread(down_first, weight_first, pair, depth), step % 2 == 0)
        mixed = columns(x_first, edge).astype(F32) + added
        act_next.append(shift_section(mixed.astype(BF16), 1))
    return (jnp.concatenate(act_next, axis=1)[None], grad_prev[None])


def solution(mesh):
    tokens = P("section", ("node", "local"), None)
    in_specs = (
        tokens,
        tokens,
        tokens,
        tokens,
        tokens,
        tokens,
        tokens,
        P("section", "node", None, None, "local"),
        P("section", None),
        P("section", "node", None, "local"),
        P("section", "node", None, "local"),
        P("section", "node", "local", None),
    )
    return jax.shard_map(
        local, mesh=mesh, in_specs=in_specs, out_specs=(tokens, tokens), check_vma=False
    )
```

```python
import functools

import jax
import jax.numpy as jnp
from jax import lax
from jax.experimental import pallas as pl
from jax.experimental.pallas import tpu as pltpu
from jax.sharding import PartitionSpec as P

EPSILON = 1e-06
Y_SIZE = 4
LANES = 128
VMEM_BYTES = 24 * 1024 * 1024
CUT_SECOND = (4, 10, 14)
CUT_FIRST = (14, 14)
CUT_END = (12, 2)
CUT_BACK = (14, 14)
CUT_LAST = (8, 8, 6, 6)
BF16 = jnp.bfloat16
F32 = jnp.float32
FEATURES_LAST = (((1,), (1,)), ((), ()))
Z_ORDER = (0, 4, -1, 3, 1, -3, -2, 2)


def shift_y(value, by):
    count = lax.axis_size("local")
    pairs = [(i, i // Y_SIZE * Y_SIZE + (i % Y_SIZE + by) % Y_SIZE) for i in range(count)]
    return lax.ppermute(value, "local", pairs)


def shift_z(value, by):
    nodes = lax.axis_size("node")
    locals_ = lax.axis_size("local")
    depth = nodes * (locals_ // Y_SIZE)
    pairs = []
    for node in range(nodes):
        for place in range(locals_):
            z = (place // Y_SIZE) * nodes + node
            to = (z + by) % depth
            pairs.append(
                (node * locals_ + place, (to % nodes) * locals_ + to // nodes * Y_SIZE + place % Y_SIZE)
            )
    return lax.ppermute(value, ("node", "local"), pairs)


def shift_section(value, by):
    size = lax.axis_size("section")
    return lax.ppermute(value, "section", [(i, (i + by) % size) for i in range(size)])


def hold(value, *marks):
    marks = [mark for mark in marks if mark is not None]
    return lax.optimization_barrier((value, marks))[0] if marks else value


def back(items, count):
    return items[-count] if len(items) >= count else None


def rms_scale(values):
    return lax.rsqrt(jnp.mean(values * values, axis=-1, keepdims=True) + EPSILON)


def cut(width, shares):
    units = width // LANES
    total = sum(shares)
    edges = [round(units * sum(shares[:i]) / total) * LANES for i in range(len(shares) + 1)]
    return list(zip(edges[:-1], edges[1:]))


def tile_of(width):
    units = width // LANES
    return LANES * max(i for i in range(1, 8) if units % i == 0)


def params():
    return pltpu.CompilerParams(vmem_limit_bytes=VMEM_BYTES)


def cost(flops, moved):
    return pl.CostEstimate(flops=flops, bytes_accessed=moved, transcendentals=0)


def opening_kernel(edges, route_f, weight_f, route_b, weight_b, rows, *outs):
    count = rows.shape[0]
    lane = lax.broadcasted_iota(jnp.int32, (count, LANES), 1)
    earlier = (
        lax.broadcasted_iota(jnp.int32, (count, count), 1)
        < lax.broadcasted_iota(jnp.int32, (count, count), 0)
    ).astype(BF16)
    kind = lane // 4
    meta = jnp.zeros((count, LANES), F32)
    for start, route, weight in ((0, route_f, weight_f), (4, route_b, weight_b)):
        first = route[:, 0:1] == lane % 4
        second = route[:, 1:2] == lane % 4
        chosen = jnp.where(first, 1.0, jnp.where(second, 1.0, 0.0))
        before = jnp.dot(earlier, chosen.astype(BF16), preferred_element_type=F32)
        value = jnp.where(first, weight[:, 0:1], jnp.where(second, weight[:, 1:2], 0.0))
        high = value.astype(BF16).astype(F32)
        middle = (value - high).astype(BF16).astype(F32)
        low = value - high - middle
        meta = jnp.where(kind == start, jnp.where(chosen > 0.0, before, -1.0), meta)
        meta = jnp.where(kind == start + 1, high, meta)
        meta = jnp.where(kind == start + 2, middle, meta)
        meta = jnp.where(kind == start + 3, low, meta)
    for i, ((low_edge, high_edge), out) in enumerate(zip(edges, outs)):
        span = high_edge - low_edge
        out[:, :span] = rows[:, low_edge:high_edge]
        if i == 0:
            out[:, span:] = meta.astype(BF16)


def opening(edges, route_f, weight_f, route_b, weight_b, rows):
    count = rows.shape[0]
    shapes = [
        jax.ShapeDtypeStruct((count, high - low + (LANES if i == 0 else 0)), BF16)
        for i, (low, high) in enumerate(edges)
    ]
    return pl.pallas_call(
        functools.partial(opening_kernel, edges),
        out_shape=shapes,
        compiler_params=params(),
        cost_estimate=cost(0, 4 * rows.size),
    )(route_f, weight_f, route_b, weight_b, rows)


def norm_kernel(edges, rows, gain, *outs):
    values = rows[...].astype(F32)
    normed = (values * rms_scale(values) * gain[...]).astype(BF16)
    for (low, high), out in zip(edges, outs):
        out[...] = normed[:, low:high]


def norm(edges, rows, gain):
    return pl.pallas_call(
        functools.partial(norm_kernel, edges),
        out_shape=[
            jax.ShapeDtypeStruct((rows.shape[0], high - low), BF16) for low, high in edges
        ],
        compiler_params=params(),
        cost_estimate=cost(8 * rows.size, 4 * rows.size),
    )(rows, gain)


def tables_kernel(capacity, slots, expert, z_of, *refs):
    blocks, outs = refs[:8], refs[8:]
    metas = jnp.concatenate([ref[...].astype(F32) for ref in blocks], axis=0)
    count = metas.shape[0]
    lane = lax.broadcasted_iota(jnp.int32, metas.shape, 1)
    mine = lane % 4 == expert[...]
    kind = lane // 4
    padded = outs[0].shape[0] // LANES * LANES + (LANES if outs[0].shape[0] % LANES else 0)
    places = lax.broadcasted_iota(jnp.int32, (count, padded), 1)
    for i, start in enumerate((0, 4)):
        slot = jnp.sum(jnp.where(mine & (kind == start), metas, 0.0), axis=1, keepdims=True)
        high = mine & (kind > start) & (kind < start + 4)
        weight = jnp.sum(jnp.where(high, metas, 0.0), axis=1, keepdims=True)
        target = jnp.where(slot >= 0.0, z_of[...] * capacity + slot.astype(jnp.int32), -1)
        down = jnp.where(target == places, 1.0, 0.0)
        across, down_out, weight_out = outs[3 * i : 3 * i + 3]
        down_out[...] = down[:, :slots].astype(BF16)
        across[...] = down.T[:slots].astype(BF16)
        weight_out[...] = jnp.sum((down * weight).T, axis=1, keepdims=True)[:slots]


def tables(expert, z_of, blocks, row, column, capacity):
    count = z_of.shape[0]
    slots = capacity * len(blocks)
    step = count // len(blocks)
    one = [
        jax.ShapeDtypeStruct((slots, count), BF16),
        jax.ShapeDtypeStruct((count, slots), BF16),
        jax.ShapeDtypeStruct((slots, 1), F32),
    ]
    whole = lambda shape: pl.BlockSpec(shape, lambda i: (0, 0))
    return pl.pallas_call(
        functools.partial(tables_kernel, capacity, slots),
        grid=(1,),
        out_shape=one * 2,
        in_specs=[whole((1, LANES)), whole((count, 1))]
        + [pl.BlockSpec((step, LANES), lambda i: (row, column))] * len(blocks),
        out_specs=[whole(item.shape) for item in one * 2],
        compiler_params=params(),
        cost_estimate=cost(0, 8 * slots * count),
    )(expert, z_of, *blocks)


def select_kernel(table, scale, *refs):
    blocks, out = refs[:-1], refs[-1]
    values = jnp.concatenate([ref[...] for ref in blocks], axis=0)
    total = jnp.dot(table[...], values, preferred_element_type=F32)
    out[...] = (total * scale[...]).astype(BF16)


def select(table, scale, blocks, width, row=0, column=0):
    rows, tokens = table.shape
    tile = tile_of(width)
    step = tokens // len(blocks)
    return pl.pallas_call(
        select_kernel,
        grid=(width // tile,),
        out_shape=jax.ShapeDtypeStruct((rows, width), BF16),
        in_specs=[
            pl.BlockSpec((rows, tokens), lambda i: (0, 0)),
            pl.BlockSpec((rows, 1), lambda i: (0, 0)),
        ]
        + [pl.BlockSpec((step, tile), lambda i: (row, i + column // tile))] * len(blocks),
        out_specs=pl.BlockSpec((rows, tile), lambda i: (0, i)),
        compiler_params=params(),
        cost_estimate=cost(2 * rows * tokens * width, 2 * (rows + tokens) * width),
    )(table, scale, *blocks)


def spread_kernel(table, scale, rows, *outs):
    values = (rows[...] * scale[...]).astype(BF16)
    total = jnp.dot(table[...], values, preferred_element_type=F32).astype(BF16)
    step = table.shape[0] // len(outs)
    for i, ref in enumerate(outs):
        ref[...] = total[i * step : (i + 1) * step]


def spread(table, scale, rows, count):
    tokens, slots = table.shape
    width = rows.shape[1]
    tile = tile_of(width)
    return pl.pallas_call(
        spread_kernel,
        grid=(width // tile,),
        out_shape=[jax.ShapeDtypeStruct((tokens // count, width), BF16)] * count,
        in_specs=[
            pl.BlockSpec((tokens, slots), lambda i: (0, 0)),
            pl.BlockSpec((slots, 1), lambda i: (0, 0)),
            pl.BlockSpec((slots, tile), lambda i: (0, i)),
        ],
        out_specs=[pl.BlockSpec((tokens // count, tile), lambda i: (0, i))] * count,
        compiler_params=params(),
        cost_estimate=cost(2 * slots * tokens * width, (4 * slots + 2 * tokens) * width),
    )(table, scale, rows)


def local(
    x_fwd,
    route_fwd,
    weight_fwd,
    x_bwd,
    grad_out,
    route_bwd,
    weight_bwd,
    saved_pre,
    norm_gain,
    w_gate,
    w_up,
    w_down,
):
    experts = lax.axis_size("node")
    halves = lax.axis_size("local") // Y_SIZE
    depth = experts * halves
    tokens, width = x_fwd.shape[1:]
    units = w_gate.shape[3]
    capacity = saved_pre.shape[2] // (depth * Y_SIZE)
    group = depth * capacity
    expert = lax.axis_index("node")
    place = lax.axis_index("local")
    my_y = place % Y_SIZE
    my_z = place // Y_SIZE * experts + expert
    gain = norm_gain[0]
    upstream = grad_out[0]

    def columns(value, edge):
        return value[:, edge[0] : edge[1]]

    cuts_second = cut(width, CUT_SECOND)
    cuts_first = cut(width, CUT_FIRST)
    cuts_back = cut(width, CUT_BACK)
    cuts_last = cut(width, CUT_LAST)
    blocks = opening(
        cuts_second, route_fwd[0], weight_fwd[0], route_bwd[0], weight_bwd[0], upstream
    )
    expert_row = jnp.full((1, LANES), expert, jnp.int32)
    z_of = jnp.concatenate(
        [jnp.full((tokens, 1), (my_z + i + depth) % depth, jnp.int32) for i in Z_ORDER], axis=0
    )
    ones = jnp.ones((group, 1), F32)

    firsts, thirds, starts, turns = [], [], [], []

    def open_z(block):
        block = hold(block, back(firsts, 1), back(starts, 2))
        got = {0: block, -1: shift_z(block, 1), 1: shift_z(block, -1)}
        firsts.append((got[-1], got[1]))
        return got

    def close_z(got, flip, *marks):
        got[-1], got[1] = hold((got[-1], got[1]), back(thirds, 1))
        for step in range(2, 5):
            if step == 3:
                got[-2], got[2] = hold((got[-2], got[2]), *marks)
            if step < 4 or not flip:
                got[-step] = shift_z(got[1 - step], 1)
            if step < 4 or flip:
                got[step] = shift_z(got[step - 1], -1)
        thirds.append((got[-3], got[3]))
        got[4] = got[4] if flip else got[-4]
        return [got[i] for i in Z_ORDER]

    def gather_y(block, *marks):
        block = hold(block, back(starts, 2), back(turns, 2), *marks)
        before = shift_y(block, 1)
        after = shift_y(block, -1)
        starts.append((before, after))
        return block, before, after

    def finish_y(parts, flip, *marks):
        block, before, after = parts
        first = hold(after if flip else before, *marks)
        far = shift_y(first, -1 if flip else 1)
        turns.append(far)
        return {0: block, -1: before, 1: after, 2: far}

    block = blocks[0]
    direct = [block if i == 0 else shift_z(block, -i) for i in Z_ORDER]
    firsts.append((direct[2], direct[4]))
    x_first = x_fwd[0]
    blocks += norm(cuts_first, hold(x_first, direct[2]), gain.reshape(1, width))
    across_first, down_first, weight_first, across_second, down_second, weight_second = tables(
        expert_row, z_of, direct, 0, cuts_second[0][1] // LANES, capacity
    )

    count_second = len(cuts_second)
    arrived, opened = [], None
    for c, (low, high) in enumerate(cuts_second + cuts_first[:1]):
        flip = c % 2 == 1
        upcoming = open_z(blocks[c + 1])
        parts = close_z(opened, flip, starts[0] if c == 1 else None) if c else direct
        opened = upcoming
        if c < count_second:
            rows = select(across_second, weight_second, parts, high - low)
        else:
            rows = select(across_first, ones, parts, high - low)
        parts = gather_y(rows, None if c else firsts[-1])
        arrived.append(finish_y(parts, flip))
    parts_last = close_z(opened, count_second % 2 == 0)

    gate_w, up_w, down_w, stored_all = hold(
        (w_gate[0, 0], w_up[0, 0], w_down[0, 0], saved_pre[0, 0]), starts[1]
    )
    both_w = jnp.concatenate([gate_w, up_w], axis=1)
    saved = stored_all.reshape(halves, Y_SIZE, experts * capacity, 2, units)
    pre_grads = {}
    for r in (2, 1, -1, 0):
        hidden_grad = sum(
            lax.dot_general(
                parts[r], columns(down_w, edge), FEATURES_LAST, preferred_element_type=F32
            )
            for parts, edge in zip(arrived, cuts_second)
        )
        stored = lax.dynamic_index_in_dim(
            saved, (my_y + r + Y_SIZE) % Y_SIZE, 1, keepdims=False
        ).reshape(group, 2, units)
        gate = stored[:, 0, :].astype(F32)
        upper = stored[:, 1, :].astype(F32)
        sigma = jax.nn.sigmoid(gate)
        grad_gate = hidden_grad * upper * sigma * (1.0 + gate * (1.0 - sigma))
        grad_upper = hidden_grad * gate * sigma
        pre_grads[r] = jnp.concatenate([grad_gate, grad_upper], axis=1).astype(BF16)

    def second_term(edge, r):
        return lax.dot_general(
            pre_grads[r], both_w[edge[0] : edge[1]], FEATURES_LAST, preferred_element_type=F32
        )

    def first_term(edge, r):
        return jnp.dot(hidden[r], columns(down_w, edge), preferred_element_type=F32)

    def start_back(term, edge, side, *marks):
        far, straight = hold((term(edge, 2).astype(BF16), term(edge, -side).astype(BF16)), *marks)
        return shift_y(far, side), shift_y(straight, -side)

    def through_back(term, edge, side, far, straight):
        return shift_y((term(edge, side) + far.astype(F32)).astype(BF16), side)

    def end_back(term, edge, side, far, straight, through):
        return term(edge, 0) + through.astype(F32) + straight.astype(F32)

    def scatter_z(parts, flip, *waits):
        parts = dict(zip(Z_ORDER, parts))
        side = 1 if flip else -1
        long, short = parts[4], parts[-side * 3]
        marks = []
        for step in (3, 2, 1, 0):
            if 3 - step < len(waits):
                long, short = hold((long, short), *waits[3 - step])
            long = shift_z(long, side)
            if step < 3:
                short = shift_z(short, -side)
            marks.append((long, short))
            if step:
                long = (parts[side * step].astype(F32) + long.astype(F32)).astype(BF16)
            if 0 < step < 3:
                short = (parts[-side * step].astype(F32) + short.astype(F32)).astype(BF16)
        return parts[0].astype(F32) + long.astype(F32) + short.astype(F32), marks

    ways = (1, -1, 1, -1)
    begun = [start_back(second_term, *item) for item in zip(cuts_back, ways)]
    turned = [through_back(second_term, *item, *got) for *item, got in zip(cuts_back, ways, begun)]
    rows = [
        end_back(second_term, *item, *got, through)
        for *item, got, through in zip(cuts_back, ways, begun, turned)
    ]
    edges_first = cuts_first[:1] + cut(width - cuts_first[1][0], CUT_END)
    edges_first[1:] = [(low + cuts_first[1][0], high + cuts_first[1][0]) for low, high in edges_first[1:]]
    pending = []
    for i, (low, high) in enumerate(edges_first[1:]):
        rows_first = select(across_first, ones, parts_last, high - low, 0, low - cuts_first[1][0])
        rows_first = hold(rows_first, turned if i else begun[0])
        pending.append((rows_first, shift_y(rows_first, 1), shift_y(rows_first, -1)))

    parts = spread(down_second, ones, jnp.concatenate(rows, axis=1), depth)
    normed_grad, ring = scatter_z(parts, False)
    arrived.append(finish_y(pending[0], False))
    arrived.append(finish_y(pending[1], True))
    hidden = {}
    for r in (2, 1, -1, 0):
        both = sum(
            jnp.dot(parts[r], both_w[edge[0] : edge[1]], preferred_element_type=F32)
            for parts, edge in zip(arrived[count_second:], edges_first)
        )
        hidden[r] = (jax.nn.silu(both[:, :units]) * both[:, units:]).astype(BF16)

    opened = [
        start_back(first_term, edge, side, ring[1]) for edge, side in zip(cuts_last[:2], ways)
    ]
    opened += [
        start_back(first_term, edge, side, ring[2]) for edge, side in zip(cuts_last[2:], ways)
    ]

    x_second = x_bwd[0].astype(F32)
    scale = rms_scale(x_second)
    along = gain * normed_grad
    input_grad = (
        upstream.astype(F32)
        + scale * along
        - x_second * (scale * scale * scale) * jnp.mean(along * x_second, axis=-1, keepdims=True)
    ).astype(BF16)
    grad_prev = shift_section(input_grad, -1)

    act_next = []
    turned = [through_back(first_term, *item, *got) for *item, got in zip(cuts_last, ways, opened)]
    rows = [
        end_back(first_term, *item, *got, through)
        for *item, got, through in zip(cuts_last, ways, opened, turned)
    ]
    for step in range(2):
        pair = jnp.concatenate(rows[2 * step : 2 * step + 2], axis=1)
        edge = (cuts_last[2 * step][0], cuts_last[2 * step + 1][1])
        added, _ = scatter_z(spread(down_first, weight_first, pair, depth), step % 2 == 0)
        mixed = columns(x_first, edge).astype(F32) + added
        act_next.append(shift_section(mixed.astype(BF16), 1))
    return (jnp.concatenate(act_next, axis=1)[None], grad_prev[None])


def solution(mesh):
    tokens = P("section", ("node", "local"), None)
    in_specs = (
        tokens,
        tokens,
        tokens,
        tokens,
        tokens,
        tokens,
        tokens,
        P("section", "node", None, None, "local"),
        P("section", None),
        P("section", "node", None, "local"),
        P("section", "node", None, "local"),
        P("section", "node", "local", None),
    )
    return jax.shard_map(
        local, mesh=mesh, in_specs=in_specs, out_specs=(tokens, tokens), check_vma=False
    )
```
